32 devices in a mesh: row: 8 (over z, core), col: 4 (over y, x).
Axes of the slice: x: 2, y: 2, z: 4, core: 2. Of those that a mesh axis runs over, the one named last changes fastest.
Arguments:
- design: bfloat16 [1024, 26624], P('row', 'col'), may hold values from -0.5 to 0.5
- group_ids: int32 [1024], replicated, may hold values from 0 to 3, never falling along the last dimension, each value on 1 to 512 neighbouring positions
- filter_zeros: float32 [2], replicated, may hold values from 0.3 to 1, as said below
- filter_poles: float32 [2], replicated, may hold values from 0.8 to 1, as said below
Outputs:
- normal: float32 [26624, 26624], P('row', 'col')
The draws below stay inside these ranges and needn't reach their ends.
Inputs may be any that keep to these rules, and one draw needn't show every extreme that they name: `group_ids`: epochs in time order; group numbers never fall along time and each group is 1 to 512 epochs long. `filter_zeros`: one zero lies in [0.3, 0.7], the other within 0.2 / 1024 below 1. `filter_poles`: one pole lies in [0.8, 0.95], the other within 2 / 1024 below 1.
All inputs are finite; a program needn't handle non-finite values.
Results may differ from the reference program's by a relative error of at most 0.0022.
Values may be sent and summed in bfloat16 or wider, within the bound.
No kernel may reach another device: no remote copies, remote signals or barrier semaphores. Data moves between devices by JAX's collectives and lax.ppermute only.
A program may use at most 192 MiB of HBM per device.

```python
import math
import jax
import jax.numpy as jnp
import numpy as np
from jax import lax

K = 26624
EPOCH_DEV = 128
GROUPS = 4
E = 1024


def ordered_pair(key, fast_value, slow_value):
    flip = jax.random.randint(jax.random.fold_in(key, 7), (), 0, 2)
    return jnp.where(flip == 1, jnp.stack([slow_value, fast_value]), jnp.stack([fast_value, slow_value])).astype(jnp.float32)


def draw_filter_zeros(key, part):
    own_key = jax.random.fold_in(key, 11)
    uniform = jax.random.uniform(own_key, (2,), jnp.float32)
    fast_value = 0.3 + 0.4 * uniform[0]
    slow_value = 1.0 - (0.05 + 0.15 * uniform[1]) / E
    return ordered_pair(own_key, fast_value, slow_value)


def draw_filter_poles(key, part):
    own_key = jax.random.fold_in(key, 23)
    uniform = jax.random.uniform(own_key, (2,), jnp.float32)
    fast_value = 0.8 + 0.15 * uniform[0]
    slow_value = 1.0 - (0.5 + 1.5 * uniform[1]) / E
    return ordered_pair(own_key, fast_value, slow_value)


def level_of(key, extent, split, low, high):
    level = 1.0
    for position, parts in split:
        draws = jax.random.uniform(jax.random.fold_in(jax.random.fold_in(key, 6), position), (parts,), jnp.float32, low / len(split), high / len(split))
        level = level * jnp.repeat(jnp.exp(draws), extent[position] // parts).reshape((-1,) + (1,) * (len(extent) - 1 - position))
    return level


def profile(amount, total, limit, skew):
    portions = [(1 << 20) // math.isqrt(grade ** skew) + 1 for grade in range(2, amount + 1)]
    spare, holding = total - limit - (amount - 1), [1] * (amount - 1)
    while spare > 0:
        movable = [i for i in range(amount - 1) if holding[i] < limit]
        pool, remaining = sum([portions[i] for i in movable]), spare
        for i in movable:
            addition = min(limit - holding[i], max(1, remaining * portions[i] // pool), spare)
            holding[i] = holding[i] + addition
            spare = spare - addition
    return np.array([limit] + holding)


def ragged_sizes(rng, number_of, total, bound, slope):
    if number_of == 2:
        one = jax.random.randint(rng, (), max(1, total - bound), min(bound, total - 1) + 1)
        return jnp.stack([one, total - one])
    lengths = jnp.asarray(profile(number_of, total, bound, slope), jnp.int32)
    pairs = (number_of - 1) // 2
    giver, sink = lengths[1:1 + 2 * pairs:2], lengths[2:2 + 2 * pairs:2]
    slack = jnp.minimum(giver - 1, bound - sink)
    passed = jax.random.randint(jax.random.fold_in(rng, 1), (pairs,), 0, 1 << 20) % (slack + 1)
    lengths = lengths.at[1:1 + 2 * pairs:2].set(giver - passed).at[2:2 + 2 * pairs:2].set(sink + passed)
    return lengths[jax.random.permutation(jax.random.fold_in(rng, 2), number_of)]


def centred(rng, shape, scale, most, pieces=(), dtype=jnp.bfloat16):
    array = scale * jax.random.normal(rng, shape, jnp.float32)
    if pieces:
        array = array * level_of(rng, shape, pieces, -0.22, 0.18)
    return jnp.clip(array, -most, most).astype(dtype)


def setup_inputs(seed: int = 0) -> dict:
    splits = jax.random.split(jax.random.key(seed), 5)
    return {
        "design": centred(splits[0], (E, K), EPOCH_DEV ** -0.5, 0.5, ((0, 8), (1, 4))),
        "group_ids": jnp.searchsorted(jnp.cumsum(ragged_sizes(splits[1], GROUPS, E, E // 2, 2)), jnp.arange(E), side="right").astype(jnp.int32),
        "filter_zeros": draw_filter_zeros(jax.random.fold_in(splits[4], 71), 0),
        "filter_poles": draw_filter_poles(jax.random.fold_in(splits[4], 71), 0),
    }


def reference(design, group_ids, filter_zeros, filter_poles):
    first_lag = -(filter_zeros[0] + filter_zeros[1])
    second_lag = filter_zeros[0] * filter_zeros[1]
    pole_sum = filter_poles[0] + filter_poles[1]
    pole_product = filter_poles[0] * filter_poles[1]
    linked = jnp.concatenate([jnp.zeros((1,), jnp.float32), (group_ids[1:] == group_ids[:-1]).astype(jnp.float32)])
    linked_two = jnp.concatenate([jnp.zeros((2,), jnp.float32), (group_ids[2:] == group_ids[:-2]).astype(jnp.float32)])
    values = design.astype(jnp.float32)
    width = values.shape[1]
    shifted_one = jnp.concatenate([jnp.zeros((1, width), jnp.float32), values[:-1]])
    shifted_two = jnp.concatenate([jnp.zeros((2, width), jnp.float32), values[:-2]])
    driven = values + (first_lag * linked)[:, None] * shifted_one + (second_lag * linked_two)[:, None] * shifted_two

    def advance(carried, inputs):
        previous, older = carried
        driven_row, link_one, link_two = inputs
        current = driven_row + pole_sum * link_one * previous - pole_product * link_two * older
        return (current, previous), current

    start_state = (jnp.zeros((width,), jnp.float32), jnp.zeros((width,), jnp.float32))
    unused, whitened = lax.scan(advance, start_state, (driven, linked, linked_two))
    whitened = whitened.astype(jnp.bfloat16)
    return lax.dot_general(whitened, whitened, (((0,), (0,)), ((), ())), preferred_element_type=jnp.float32)
```

```python
import functools

import jax
import jax.numpy as jnp
from jax import lax
from jax.experimental import pallas as pl
from jax.experimental.pallas import tpu as pltpu
from jax.sharding import PartitionSpec as P

VMEM_BYTES = 56 * 1024 * 1024
COLUMN_UNITS = (6, 5, 2)
ROW_UNITS = (3, 3, 4, 3)


def block_matrices(group_ids, filter_zeros, filter_poles, rows):
    p, z = filter_poles, filter_zeros
    share = jnp.stack(
        [
            (p[0] - z[0]) * (p[0] - z[1]) / (p[0] - p[1]),
            (p[1] - z[0]) * (p[1] - z[1]) / (p[1] - p[0]),
        ]
    )
    g = group_ids.reshape(rows, -1)
    length = g.shape[1]
    i = jnp.arange(length, dtype=jnp.int32)
    powers = p[:, None] ** jnp.arange(length + 1, dtype=jnp.float32)[None, :]
    lag = i[:, None] - i[None, :]
    ahead = jnp.maximum(lag - 1, 0).astype(jnp.float32)
    response = jnp.where(lag == 0, 1.0, share[0] * p[0] ** ahead + share[1] * p[1] ** ahead)
    same = (g[:, :, None] == g[:, None, :]) & (lag >= 0)
    inside = jnp.where(same, response, 0.0)
    left = (length - 1 - i).astype(jnp.float32)
    ends = share[:, None] * p[:, None] ** left[None, :]
    ends = jnp.where((g == g[:, -1:])[:, None, :], ends[None], 0.0)
    matrix = jnp.concatenate([inside, jnp.pad(ends, ((0, 0), (0, 14), (0, 0)))], axis=1)
    high = lax.reduce_precision(matrix, 8, 7)
    matrix = jnp.concatenate([high, matrix - high], axis=2).astype(jnp.bfloat16)
    before = jnp.concatenate([jnp.full((1,), -1, jnp.int32), g[:-1, -1]])
    reached = (g == before[:, None]).astype(jnp.float32)
    gains = reached[:, :, None] * powers[:, :length].T[None]
    keep = reached[:, -1:, None] * powers[:, length][None, None, :]
    gains = jnp.concatenate([gains, jnp.broadcast_to(keep, gains.shape)], axis=2)
    return matrix, jnp.pad(gains, ((0, 0), (0, 0), (0, 4)))


def whiten_blocks(rows, blocks, matrix, gains, put):
    one = two = None
    for b in range(rows):
        block = blocks(b)
        length = block.shape[0]
        full = jnp.dot(
            matrix[b], jnp.concatenate([block, block], axis=0), preferred_element_type=jnp.float32
        )
        values = full[:length]
        ends = full[length : length + 1], full[length + 1 : length + 2]
        if b > 0:
            values = values + gains[b, :, 0:1] * one + gains[b, :, 1:2] * two
            ends = ends[0] + gains[b, 0:1, 2:3] * one, ends[1] + gains[b, 0:1, 3:4] * two
        one, two = ends
        put(b, values.astype(jnp.bfloat16))


def whiten_columns_kernel(rows, core, raw, matrix, gains, panel):
    length = raw.shape[0] // rows

    def put(b, values):
        panel[b * length : (b + 1) * length, :] = values

    whiten_blocks(rows, lambda b: raw[b * length : (b + 1) * length, :], matrix, gains, put)


def tile_of(width):
    return next(t for t in (512, 384, 256, 128) if width % t == 0)


def whiten_columns(core, raw, width, matrix, gains):
    epochs, rows, tile = raw.shape[0], matrix.shape[0], tile_of(width)
    tiles = width // tile
    whole = lambda a: pl.BlockSpec(a.shape, lambda i, s: (0, 0, 0))
    return pl.pallas_call(
        functools.partial(whiten_columns_kernel, rows),
        grid_spec=pltpu.PrefetchScalarGridSpec(
            num_scalar_prefetch=1,
            grid=(tiles,),
            in_specs=[pl.BlockSpec((epochs, tile), lambda i, s: (0, s[0] * tiles + i)), whole(matrix), whole(gains)],
            out_specs=pl.BlockSpec((epochs, tile), lambda i, s: (0, i)),
        ),
        out_shape=jax.ShapeDtypeStruct((epochs, width), jnp.bfloat16),
        compiler_params=pltpu.CompilerParams(vmem_limit_bytes=VMEM_BYTES),
        cost_estimate=pl.CostEstimate(
            flops=8 * 144 * 256 * rows * width, bytes_accessed=4 * epochs * width, transcendentals=0
        ),
        name="whiten_columns",
    )(core, raw, matrix, gains)


def whiten_rows_kernel(rows, slots, place, raw, matrix, gains, turned, held):
    core, chip, col = place[0], place[1], place[2]
    chips, shares = rows // 2, len(slots)
    share = raw.shape[1]
    length = share * shares

    def blocks(b):
        parts = []
        for s in range(shares):
            away = jnp.bitwise_xor(col, s)
            slot = sum(jnp.where(away == d, slots[d], 0) for d in range(shares))
            at = slot * rows + jnp.bitwise_xor(core, b % 2) * chips + jnp.bitwise_xor(chip, b // 2)
            parts.append(raw[at])
        return jnp.concatenate(parts, axis=0)

    def put(b, values):
        held[b * length : (b + 1) * length, :] = values

    whiten_blocks(rows, blocks, matrix, gains, put)
    turned[...] = held[...].T


def whiten_rows(place, raw, slots, matrix, gains):
    count, share, width = raw.shape
    epochs, rows, tile = count * share, matrix.shape[0], tile_of(width)
    whole = lambda a: pl.BlockSpec(a.shape, lambda i, s: (0, 0, 0))
    return pl.pallas_call(
        functools.partial(whiten_rows_kernel, rows, slots),
        grid_spec=pltpu.PrefetchScalarGridSpec(
            num_scalar_prefetch=1,
            grid=(width // tile,),
            in_specs=[pl.BlockSpec((count, share, tile), lambda i, s: (0, 0, i)), whole(matrix), whole(gains)],
            out_specs=pl.BlockSpec((tile, epochs), lambda i, s: (i, 0)),
            scratch_shapes=[pltpu.VMEM((epochs, tile), jnp.bfloat16)],
        ),
        out_shape=jax.ShapeDtypeStruct((width, epochs), jnp.bfloat16),
        compiler_params=pltpu.CompilerParams(vmem_limit_bytes=VMEM_BYTES),
        cost_estimate=pl.CostEstimate(
            flops=8 * 144 * 256 * rows * width, bytes_accessed=4 * epochs * width, transcendentals=0
        ),
        name="whiten_rows",
    )(place, raw, matrix, gains)


def product_kernel(first_row, heights, wides, sub, chained, core, *refs):
    n, m = len(heights), len(wides)
    piece_refs, column_refs = refs[:n], refs[n : n + m]
    out = refs[n + m + chained]
    rest = refs[n + m + chained + 1 :]
    held, wide, stage = rest[:n], rest[n : n + m], rest[n + m]
    piece_sem, column_sem, stage_sem = rest[n + m + 1 :]
    pieces = [pltpu.make_async_copy(piece_refs[i], held[i], piece_sem.at[i]) for i in range(n)]
    columns = [pltpu.make_async_copy(column_refs[j], wide[j], column_sem.at[j]) for j in range(m)]
    pieces[0].start()
    for copy in columns + pieces[1:]:
        copy.start()
    flying = [None, None]
    turn = 0
    row = first_row
    for i, height in enumerate(heights):
        pieces[i].wait()
        for j, (own, start, width) in enumerate(wides):
            if i == 0:
                columns[j].wait()
            slot = turn % 2
            if flying[slot] is not None:
                flying[slot].wait()
            stage[slot, :height, :width] = jnp.dot(
                held[i][...], wide[j][...], preferred_element_type=jnp.float32
            )
            home = core[0] if own else 1 - core[0]
            flying[slot] = pltpu.make_async_copy(
                stage.at[slot, pl.ds(0, height), pl.ds(0, width)],
                out.at[pl.ds(row, height), pl.ds(pl.multiple_of(home * sub + start, 128), width)],
                stage_sem.at[slot],
            )
            flying[slot].start()
            turn += 1
        row += height
    for copy in flying:
        if copy is not None:
            copy.wait()


def product(core, first_row, pieces, columns, out, shape, sub):
    heights = [p.shape[0] for p in pieces]
    wides = [(own, s, c.shape[1]) for own, s, c in columns]
    epochs = columns[0][2].shape[0]
    height, width = sum(heights), sum(w for _, _, w in wides)
    chained = int(out is not None)
    anywhere = pl.BlockSpec(memory_space=pl.ANY)
    args = list(pieces) + [c for _, _, c in columns] + ([out] if chained else [])
    return pl.pallas_call(
        functools.partial(product_kernel, first_row, heights, wides, sub, chained),
        grid_spec=pltpu.PrefetchScalarGridSpec(
            num_scalar_prefetch=1,
            grid=(),
            in_specs=[anywhere] * len(args),
            out_specs=anywhere,
            scratch_shapes=[pltpu.VMEM((h, epochs), jnp.bfloat16) for h in heights]
            + [pltpu.VMEM((epochs, w), jnp.bfloat16) for _, _, w in wides]
            + [
                pltpu.VMEM((2, max(heights), max(w for _, _, w in wides)), jnp.float32),
                pltpu.SemaphoreType.DMA((len(heights),)),
                pltpu.SemaphoreType.DMA((len(wides),)),
                pltpu.SemaphoreType.DMA((2,)),
            ],
        ),
        out_shape=jax.ShapeDtypeStruct(shape, jnp.float32),
        input_output_aliases={len(args): 0} if chained else {},
        compiler_params=pltpu.CompilerParams(vmem_limit_bytes=VMEM_BYTES),
        cost_estimate=pl.CostEstimate(
            flops=2 * epochs * height * width,
            bytes_accessed=4 * height * width + 2 * epochs * (height + width),
            transcendentals=0,
        ),
        name="product",
    )(core, *args)


def tied(values, others):
    return lax.optimization_barrier((values, others))[0]


def swapped(value, axis, distance):
    return lax.ppermute(value, axis, [(i, i ^ distance) for i in range(lax.axis_size(axis))])


def row_shares(design):
    col_count, chips = lax.axis_size("col"), lax.axis_size("row") // 2
    row, col = lax.axis_index("row"), lax.axis_index("col")
    core, chip = lax.rem(row, 2), row // 2
    share = design.shape[0] // col_count
    sub = design.shape[1] // 2
    given = lambda d: lax.dynamic_slice_in_dim(design, jnp.bitwise_xor(col, d) * share, share, 0)
    panels = jnp.stack([given(0)] + [swapped(given(d), "col", d) for d in range(1, col_count)])
    held = lambda e: lax.dynamic_index_in_dim(panels, jnp.bitwise_xor(jnp.bitwise_xor(chip, e), col), 0, False)
    mine = jnp.stack([held(0)] + [swapped(held(e), "row", 2 * e) for e in range(1, chips)])
    keep = lax.dynamic_slice_in_dim(mine, core * sub, sub, 2)
    give = lax.dynamic_slice_in_dim(mine, (1 - core) * sub, sub, 2)
    return jnp.concatenate([keep, swapped(give, "row", 1)], axis=0)


def all_shares(part, distances):
    slots = [0]
    for d in distances:
        part = jnp.concatenate([part, swapped(part, "col", d)], axis=0)
        slots = slots + [s ^ d for s in slots]
    where = [0] * len(slots)
    for slot, distance in enumerate(slots):
        where[distance] = slot
    return part, tuple(where)


def local(design, group_ids, filter_zeros, filter_poles):
    row_count, col_count = lax.axis_size("row"), lax.axis_size("col")
    row = lax.axis_index("row")
    core = lax.rem(row, 2)
    core_arg = core.reshape(1)
    place = jnp.stack([core, row // 2, lax.axis_index("col")])
    panel_width = design.shape[1]
    sub = panel_width // 2
    unit = sub // 13
    matrix, gains = block_matrices(group_ids, filter_zeros, filter_poles, row_count)

    shares = row_shares(design)
    distances = [2**k for k in range((col_count - 1).bit_length())]
    row_raws, at = [], 0
    for k, units in enumerate(ROW_UNITS):
        order = distances if k % 2 == 0 else distances[1:] + distances[:1]
        row_raws.append(all_shares(shares[:, :, at : at + units * unit], order))
        at += units * unit

    raws, at = [], 0
    for units in COLUMN_UNITS:
        end = at + units * unit
        mine = jnp.concatenate([design[:, at:end], design[:, sub + at : sub + end]], axis=1)
        if raws:
            mine = tied(mine, matrix if len(raws) == 1 else raws[-2][1])
        raws.append((at, lax.all_gather(mine, "row", axis=0, tiled=True)))
        at = end

    def columns_of(k, after=None):
        start, raw = raws[k]
        if after is not None:
            raw = tied(raw, after)
        mine = whiten_columns(core_arg, raw, COLUMN_UNITS[k] * unit, matrix, gains)
        return [(True, start, mine), (False, start, swapped(mine, "row", 1))]

    def rows_of(k, after=None):
        raw, slots = row_raws[k]
        if after is not None:
            raw = tied(raw, after)
        return whiten_rows(place, raw, slots, matrix, gains)

    shape = (sub, panel_width)
    call = lambda first, p, c, o: product(core_arg, first, p, c, o, shape, sub)
    height = sum(ROW_UNITS[:2]) * unit
    zero = columns_of(0)
    early = [rows_of(0), rows_of(1)]
    out = call(0, early, zero, None)
    late = [rows_of(2, early), rows_of(3, early)]
    out = call(height, late, zero, out)
    first = columns_of(1, late)
    out = call(0, early + late, first, out)
    second = columns_of(2, first[0][2])
    return call(0, early + late, second, out)


def solution(mesh):
    return jax.shard_map(
        local,
        mesh=mesh,
        in_specs=(P("row", "col"), P(), P(), P()),
        out_specs=P("row", "col"),
        check_vma=False,
    )
```

```python
import functools

import jax
import jax.numpy as jnp
from jax import lax
from jax.experimental import pallas as pl
from jax.experimental.pallas import tpu as pltpu
from jax.sharding import PartitionSpec as P

VMEM_BYTES = 56 * 1024 * 1024
COLUMN_UNITS = (8, 5)


def block_matrices(group_ids, filter_zeros, filter_poles, rows):
    p, z = filter_poles, filter_zeros
    share = jnp.stack(
        [
            (p[0] - z[0]) * (p[0] - z[1]) / (p[0] - p[1]),
            (p[1] - z[0]) * (p[1] - z[1]) / (p[1] - p[0]),
        ]
    )
    g = group_ids.reshape(rows, -1)
    length = g.shape[1]
    i = jnp.arange(length, dtype=jnp.int32)
    powers = p[:, None] ** jnp.arange(length + 1, dtype=jnp.float32)[None, :]
    lag = i[:, None] - i[None, :]
    ahead = jnp.maximum(lag - 1, 0).astype(jnp.float32)
    response = jnp.where(lag == 0, 1.0, share[0] * p[0] ** ahead + share[1] * p[1] ** ahead)
    same = (g[:, :, None] == g[:, None, :]) & (lag >= 0)
    inside = jnp.where(same, response, 0.0)
    left = (length - 1 - i).astype(jnp.float32)
    ends = share[:, None] * p[:, None] ** left[None, :]
    ends = jnp.where((g == g[:, -1:])[:, None, :], ends[None], 0.0)
    matrix = jnp.concatenate([inside, jnp.pad(ends, ((0, 0), (0, 14), (0, 0)))], axis=1)
    high = lax.reduce_precision(matrix, 8, 7)
    matrix = jnp.concatenate([high, matrix - high], axis=2).astype(jnp.bfloat16)
    before = jnp.concatenate([jnp.full((1,), -1, jnp.int32), g[:-1, -1]])
    reached = (g == before[:, None]).astype(jnp.float32)
    gains = reached[:, :, None] * powers[:, :length].T[None]
    keep = reached[:, -1:, None] * powers[:, length][None, None, :]
    gains = jnp.concatenate([gains, jnp.broadcast_to(keep, gains.shape)], axis=2)
    return matrix, jnp.pad(gains, ((0, 0), (0, 0), (0, 4)))


def whiten_blocks(rows, blocks, matrix, gains, put):
    one = two = None
    for b in range(rows):
        block = blocks(b)
        length = block.shape[0]
        full = jnp.dot(
            matrix[b], jnp.concatenate([block, block], axis=0), preferred_element_type=jnp.float32
        )
        values = full[:length]
        ends = full[length : length + 1], full[length + 1 : length + 2]
        if b > 0:
            values = values + gains[b, :, 0:1] * one + gains[b, :, 1:2] * two
            ends = ends[0] + gains[b, 0:1, 2:3] * one, ends[1] + gains[b, 0:1, 3:4] * two
        one, two = ends
        put(b, values.astype(jnp.bfloat16))


def tile_of(width):
    return width if width <= 1024 else next(t for t in (1024, 896, 768, 640, 512, 256, 128) if width % t == 0)


def whiten_columns_kernel(rows, core, raw, matrix, gains, panel):
    length = raw.shape[0] // rows

    def put(b, values):
        panel[b * length : (b + 1) * length, :] = values

    whiten_blocks(rows, lambda b: raw[b * length : (b + 1) * length, :], matrix, gains, put)


def whiten_columns(core, raw, width, matrix, gains):
    epochs, rows, tile = raw.shape[0], matrix.shape[0], tile_of(width)
    tiles = width // tile
    whole = lambda a: pl.BlockSpec(a.shape, lambda i, s: (0, 0, 0))
    return pl.pallas_call(
        functools.partial(whiten_columns_kernel, rows),
        grid_spec=pltpu.PrefetchScalarGridSpec(
            num_scalar_prefetch=1,
            grid=(tiles,),
            in_specs=[pl.BlockSpec((epochs, tile), lambda i, s: (0, s[0] * tiles + i)), whole(matrix), whole(gains)],
            out_specs=pl.BlockSpec((epochs, tile), lambda i, s: (0, i)),
        ),
        out_shape=jax.ShapeDtypeStruct((epochs, width), jnp.bfloat16),
        compiler_params=pltpu.CompilerParams(vmem_limit_bytes=VMEM_BYTES),
        cost_estimate=pl.CostEstimate(
            flops=8 * 144 * 256 * rows * width, bytes_accessed=4 * epochs * width, transcendentals=0
        ),
        name="whiten_columns",
    )(core, raw, matrix, gains)


def whiten_rows_kernel(rows, place, raw, matrix, gains, turned, held):
    core, chip = place[0], place[1]
    chips, length = rows // 2, raw.shape[1]

    def blocks(b):
        return raw[jnp.bitwise_xor(core, b % 2) * chips + jnp.bitwise_xor(chip, b // 2)]

    def put(b, values):
        held[b * length : (b + 1) * length, :] = values

    whiten_blocks(rows, blocks, matrix, gains, put)
    turned[...] = held[...].T


def whiten_rows(place, raw, width, matrix, gains):
    rows, length, tile = matrix.shape[0], raw.shape[1], tile_of(width)
    epochs = rows * length
    whole = lambda a: pl.BlockSpec(a.shape, lambda i, s: (0, 0, 0))
    return pl.pallas_call(
        functools.partial(whiten_rows_kernel, rows),
        grid_spec=pltpu.PrefetchScalarGridSpec(
            num_scalar_prefetch=1,
            grid=(width // tile,),
            in_specs=[pl.BlockSpec((rows, length, tile), lambda i, s: (0, 0, i)), whole(matrix), whole(gains)],
            out_specs=pl.BlockSpec((tile, epochs), lambda i, s: (i, 0)),
            scratch_shapes=[pltpu.VMEM((epochs, tile), jnp.bfloat16)],
        ),
        out_shape=jax.ShapeDtypeStruct((width, epochs), jnp.bfloat16),
        compiler_params=pltpu.CompilerParams(vmem_limit_bytes=VMEM_BYTES),
        cost_estimate=pl.CostEstimate(
            flops=8 * 144 * 256 * rows * width, bytes_accessed=4 * epochs * width, transcendentals=0
        ),
        name="whiten_rows",
    )(place, raw, matrix, gains)


def product_kernel(parts, wides, pairs, sub, chained, place, *refs):
    n, m = len(parts), len(wides)
    piece_refs, column_refs = refs[:n], refs[n : n + m]
    out = refs[n + m + chained]
    rest = refs[n + m + chained + 1 :]
    held, wide, stage = rest[:n], rest[n : n + m], rest[n + m]
    piece_sem, column_sem, stage_sem = rest[n + m + 1 :]
    loads = {}
    for i, j in pairs:
        if ("piece", i) not in loads:
            loads["piece", i] = pltpu.make_async_copy(piece_refs[i], held[i], piece_sem.at[i])
        if ("wide", j) not in loads:
            loads["wide", j] = pltpu.make_async_copy(column_refs[j], wide[j], column_sem.at[j])
    for copy in loads.values():
        copy.start()
    slots = stage.shape[0]
    flying = [None] * slots
    turn = 0
    for i, j in pairs:
        for key in (("piece", i), ("wide", j)):
            if key in loads:
                loads.pop(key).wait()
        own, start, width = wides[j]
        home = place[0] if own else 1 - place[0]
        column = pl.multiple_of(home * sub + start, 128)
        for at, size, entry in parts[i]:
            slot = turn % slots
            if flying[slot] is not None:
                flying[slot].wait()
            stage[slot, :size, :width] = jnp.dot(
                held[i][at : at + size, :], wide[j][...], preferred_element_type=jnp.float32
            )
            flying[slot] = pltpu.make_async_copy(
                stage.at[slot, pl.ds(0, size), pl.ds(0, width)],
                out.at[pl.ds(pl.multiple_of(place[entry], 64), size), pl.ds(column, width)],
                stage_sem.at[slot],
            )
            flying[slot].start()
            turn += 1
    for copy in flying:
        if copy is not None:
            copy.wait()


def product(place, pieces, columns, pairs, out, shape, sub):
    parts = [segments for segments, _ in pieces]
    heights = [p.shape[0] for _, p in pieces]
    wides = [(own, s, c.shape[1]) for own, s, c in columns]
    epochs = columns[0][2].shape[0]
    done = sum(heights[i] * wides[j][2] for i, j in pairs)
    chained = int(out is not None)
    anywhere = pl.BlockSpec(memory_space=pl.ANY)
    args = [p for _, p in pieces] + [c for _, _, c in columns] + ([out] if chained else [])
    tall, broad = max(size for p in parts for _, size, _ in p), max(w for _, _, w in wides)
    return pl.pallas_call(
        functools.partial(product_kernel, parts, wides, pairs, sub, chained),
        grid_spec=pltpu.PrefetchScalarGridSpec(
            num_scalar_prefetch=1,
            grid=(),
            in_specs=[anywhere] * len(args),
            out_specs=anywhere,
            scratch_shapes=[pltpu.VMEM((h, epochs), jnp.bfloat16) for h in heights]
            + [pltpu.VMEM((epochs, w), jnp.bfloat16) for _, _, w in wides]
            + [
                pltpu.VMEM((3, tall, broad), jnp.float32),
                pltpu.SemaphoreType.DMA((len(heights),)),
                pltpu.SemaphoreType.DMA((len(wides),)),
                pltpu.SemaphoreType.DMA((3,)),
            ],
        ),
        out_shape=jax.ShapeDtypeStruct(shape, jnp.float32),
        input_output_aliases={len(args): 0} if chained else {},
        compiler_params=pltpu.CompilerParams(vmem_limit_bytes=VMEM_BYTES),
        cost_estimate=pl.CostEstimate(
            flops=2 * epochs * done,
            bytes_accessed=4 * done + 2 * epochs * (sum(heights) + sum(w for _, _, w in wides)),
            transcendentals=0,
        ),
        name="product",
    )(place, *args)


def tied(values, others):
    return lax.optimization_barrier((values, others))[0]


def swapped(value, axis, distance):
    return lax.ppermute(value, axis, [(i, i ^ distance) for i in range(lax.axis_size(axis))])


def share_start(index, share, sub):
    return jnp.minimum(index * share, sub - share)


def row_share(design, share):
    col_count, chips = lax.axis_size("col"), lax.axis_size("row") // 2
    row, col = lax.axis_index("row"), lax.axis_index("col")
    core, chip = lax.rem(row, 2), row // 2
    sub = design.shape[1] // 2

    def given(d):
        start = share_start(jnp.bitwise_xor(col, d), share, sub)
        return jnp.concatenate(
            [lax.dynamic_slice_in_dim(design, h * sub + start, share, 1) for h in range(2)], axis=1
        )

    panels = jnp.stack([given(0)] + [swapped(given(d), "col", d) for d in range(1, col_count)])
    held = lambda e: lax.dynamic_index_in_dim(panels, jnp.bitwise_xor(jnp.bitwise_xor(chip, e), col), 0, False)
    mine = jnp.stack([held(0)] + [swapped(held(e), "row", 2 * e) for e in range(1, chips)])
    keep = lax.dynamic_slice_in_dim(mine, core * share, share, 2)
    give = lax.dynamic_slice_in_dim(mine, (1 - core) * share, share, 2)
    return jnp.concatenate([keep, swapped(give, "row", 1)], axis=0)


def all_shares(part, first, order):
    held, away, steps = part, [0], [([order[0]], first)]
    for k, d in enumerate(order):
        new, far = (first if k == 0 else swapped(held, "col", d)), [a ^ d for a in away]
        if k > 0:
            steps.append((far, new))
        if k + 1 < len(order):
            held, away = jnp.concatenate([held, new], axis=0), away + far
    return steps


def local(design, group_ids, filter_zeros, filter_poles):
    row_count, col_count = lax.axis_size("row"), lax.axis_size("col")
    row, col = lax.axis_index("row"), lax.axis_index("col")
    core = lax.rem(row, 2)
    panel_width = design.shape[1]
    sub = panel_width // 2
    unit = sub // 13
    share = -(-sub // (128 * col_count)) * 128
    distances = [2**k for k in range((col_count - 1).bit_length())]
    starts = [share_start(jnp.bitwise_xor(col, d), share, sub) + p * (share // 2) for p in range(2) for d in range(col_count)]
    place = jnp.stack([core, row // 2] + starts).astype(jnp.int32)
    entry = lambda distance, part: 2 + part * col_count + distance
    matrix, gains = block_matrices(group_ids, filter_zeros, filter_poles, row_count)

    core_arg = core.reshape(1)
    raws, at = [], 0
    for units in COLUMN_UNITS:
        end = at + units * unit
        mine = jnp.concatenate([design[:, at:end], design[:, sub + at : sub + end]], axis=1)
        if raws:
            mine = tied(mine, matrix)
        raws.append((at, lax.all_gather(mine, "row", axis=0, tiled=True)))
        at = end

    turned = whiten_rows(place, row_share(design, share), share, matrix, gains)
    half = share // 2
    orders = [distances[p:] + distances[:p] for p in range(2)]
    parts = [turned[p * half : (p + 1) * half] for p in range(2)]
    firsts = [swapped(parts[p], "col", orders[p][0]) for p in range(2)]

    def columns_of(k, after):
        start, raw = raws[k]
        mine = whiten_columns(core_arg, tied(raw, after), COLUMN_UNITS[k] * unit, matrix, gains)
        return (True, start, mine), (False, start, swapped(mine, "row", 1))

    shape = (sub, panel_width)
    own, others = columns_of(0, turned)
    whole = ([(0, half, entry(0, 0)), (half, half, entry(0, 1))], turned)
    out = product(place, [whole], [own], [(0, 0)], None, shape, sub)
    out, firsts = lax.optimization_barrier((out, firsts))
    steps = [all_shares(parts[p], firsts[p], orders[p]) for p in range(2)]
    groups = [[whole]]
    for k in range(len(distances)):
        group = []
        for p in range(2):
            far, new = steps[p][k]
            group.append(([(s * half, half, entry(d, p)) for s, d in enumerate(far)], new))
        groups.append(group)

    early = [piece for group in groups[:-1] for piece in group]
    pairs = [(0, 1)] + [(i, j) for i in range(1, len(early)) for j in range(2)]
    out = product(place, early, [own, others], pairs, out, shape, sub)
    out, raw = lax.optimization_barrier((out, raws[1][1]))
    raws[1] = (raws[1][0], raw)
    more = columns_of(1, own[2])
    late = groups[-1]
    out, mine = lax.optimization_barrier((out, more[0][2]))
    more = ((True, more[0][1], mine), more[1])
    out = product(place, late, [own, others], [(i, j) for j in range(2) for i in range(len(late))], out, shape, sub)
    every = early + late
    return product(place, every, more, [(i, j) for j in range(2) for i in range(len(every))], out, shape, sub)


def solution(mesh):
    return jax.shard_map(
        local,
        mesh=mesh,
        in_specs=(P("row", "col"), P(), P(), P()),
        out_specs=P("row", "col"),
        check_vma=False,
    )
```

```python
import functools

import jax
import jax.numpy as jnp
from jax import lax
from jax.experimental import pallas as pl
from jax.experimental.pallas import tpu as pltpu
from jax.sharding import PartitionSpec as P

VMEM_BYTES = 56 * 1024 * 1024
COLUMN_UNITS = (8, 5)


def block_matrices(group_ids, filter_zeros, filter_poles, rows):
    p, z = filter_poles, filter_zeros
    share = jnp.stack(
        [
            (p[0] - z[0]) * (p[0] - z[1]) / (p[0] - p[1]),
            (p[1] - z[0]) * (p[1] - z[1]) / (p[1] - p[0]),
        ]
    )
    g = group_ids.reshape(rows, -1)
    length = g.shape[1]
    i = jnp.arange(length, dtype=jnp.int32)
    powers = p[:, None] ** jnp.arange(length + 1, dtype=jnp.float32)[None, :]
    lag = i[:, None] - i[None, :]
    ahead = jnp.maximum(lag - 1, 0).astype(jnp.float32)
    response = jnp.where(lag == 0, 1.0, share[0] * p[0] ** ahead + share[1] * p[1] ** ahead)
    same = (g[:, :, None] == g[:, None, :]) & (lag >= 0)
    inside = jnp.where(same, response, 0.0)
    left = (length - 1 - i).astype(jnp.float32)
    ends = share[:, None] * p[:, None] ** left[None, :]
    ends = jnp.where((g == g[:, -1:])[:, None, :], ends[None], 0.0)
    matrix = jnp.concatenate([inside, jnp.pad(ends, ((0, 0), (0, 14), (0, 0)))], axis=1)
    high = lax.reduce_precision(matrix, 8, 7)
    matrix = jnp.concatenate([high, matrix - high], axis=2).astype(jnp.bfloat16)
    before = jnp.concatenate([jnp.full((1,), -1, jnp.int32), g[:-1, -1]])
    reached = (g == before[:, None]).astype(jnp.float32)
    gains = reached[:, :, None] * powers[:, :length].T[None]
    keep = reached[:, -1:, None] * powers[:, length][None, None, :]
    gains = jnp.concatenate([gains, jnp.broadcast_to(keep, gains.shape)], axis=2)
    return matrix, jnp.pad(gains, ((0, 0), (0, 0), (0, 4)))


def whiten_blocks(rows, blocks, matrix, gains, put):
    one = two = None
    for b in range(rows):
        block = blocks(b)
        length = block.shape[0]
        full = jnp.dot(
            matrix[b], jnp.concatenate([block, block], axis=0), preferred_element_type=jnp.float32
        )
        values = full[:length]
        ends = full[length : length + 1], full[length + 1 : length + 2]
        if b > 0:
            values = values + gains[b, :, 0:1] * one + gains[b, :, 1:2] * two
            ends = ends[0] + gains[b, 0:1, 2:3] * one, ends[1] + gains[b, 0:1, 3:4] * two
        one, two = ends
        put(b, values.astype(jnp.bfloat16))


def tile_of(width):
    return width if width <= 1024 else next(t for t in (1024, 896, 768, 640, 512, 256, 128) if width % t == 0)


def whiten_columns_kernel(rows, core, raw, matrix, gains, panel):
    length = raw.shape[0] // rows

    def put(b, values):
        panel[b * length : (b + 1) * length, :] = values

    whiten_blocks(rows, lambda b: raw[b * length : (b + 1) * length, :], matrix, gains, put)


def whiten_columns(core, raw, width, matrix, gains):
    epochs, rows, tile = raw.shape[0], matrix.shape[0], tile_of(width)
    tiles = width // tile
    whole = lambda a: pl.BlockSpec(a.shape, lambda i, s: (0, 0, 0))
    return pl.pallas_call(
        functools.partial(whiten_columns_kernel, rows),
        grid_spec=pltpu.PrefetchScalarGridSpec(
            num_scalar_prefetch=1,
            grid=(tiles,),
            in_specs=[pl.BlockSpec((epochs, tile), lambda i, s: (0, s[0] * tiles + i)), whole(matrix), whole(gains)],
            out_specs=pl.BlockSpec((epochs, tile), lambda i, s: (0, i)),
        ),
        out_shape=jax.ShapeDtypeStruct((epochs, width), jnp.bfloat16),
        compiler_params=pltpu.CompilerParams(vmem_limit_bytes=VMEM_BYTES),
        cost_estimate=pl.CostEstimate(
            flops=8 * 144 * 256 * rows * width, bytes_accessed=4 * epochs * width, transcendentals=0
        ),
        name="whiten_columns",
    )(core, raw, matrix, gains)


def whiten_rows_kernel(rows, place, raw, matrix, gains, turned, held):
    core, chip = place[0], place[1]
    chips, length = rows // 2, raw.shape[1]

    def blocks(b):
        return raw[jnp.bitwise_xor(core, b % 2) * chips + jnp.bitwise_xor(chip, b // 2)]

    def put(b, values):
        held[b * length : (b + 1) * length, :] = values

    whiten_blocks(rows, blocks, matrix, gains, put)
    turned[...] = held[...].T


def whiten_rows(place, raw, width, matrix, gains):
    rows, length, tile = matrix.shape[0], raw.shape[1], tile_of(width)
    epochs = rows * length
    whole = lambda a: pl.BlockSpec(a.shape, lambda i, s: (0, 0, 0))
    return pl.pallas_call(
        functools.partial(whiten_rows_kernel, rows),
        grid_spec=pltpu.PrefetchScalarGridSpec(
            num_scalar_prefetch=1,
            grid=(width // tile,),
            in_specs=[pl.BlockSpec((rows, length, tile), lambda i, s: (0, 0, i)), whole(matrix), whole(gains)],
            out_specs=pl.BlockSpec((tile, epochs), lambda i, s: (i, 0)),
            scratch_shapes=[pltpu.VMEM((epochs, tile), jnp.bfloat16)],
        ),
        out_shape=jax.ShapeDtypeStruct((width, epochs), jnp.bfloat16),
        compiler_params=pltpu.CompilerParams(vmem_limit_bytes=VMEM_BYTES),
        cost_estimate=pl.CostEstimate(
            flops=8 * 144 * 256 * rows * width, bytes_accessed=4 * epochs * width, transcendentals=0
        ),
        name="whiten_rows",
    )(place, raw, matrix, gains)


def product_kernel(parts, wides, pairs, sub, chained, place, *refs):
    n, m = len(parts), len(wides)
    piece_refs, column_refs = refs[:n], refs[n : n + m]
    out = refs[n + m + chained]
    rest = refs[n + m + chained + 1 :]
    held, wide, stage = rest[:n], rest[n : n + m], rest[n + m]
    piece_sem, column_sem, stage_sem = rest[n + m + 1 :]
    loads = {}
    for i, j in pairs:
        if ("piece", i) not in loads:
            loads["piece", i] = pltpu.make_async_copy(piece_refs[i], held[i], piece_sem.at[i])
        if ("wide", j) not in loads:
            loads["wide", j] = pltpu.make_async_copy(column_refs[j], wide[j], column_sem.at[j])
    for copy in loads.values():
        copy.start()
    slots = stage.shape[0]
    flying = [None] * slots
    turn = 0
    for i, j in pairs:
        for key in (("piece", i), ("wide", j)):
            if key in loads:
                loads.pop(key).wait()
        own, start, width = wides[j]
        home = place[0] if own else 1 - place[0]
        column = pl.multiple_of(home * sub + start, 128)
        for at, size, entry in parts[i]:
            slot = turn % slots
            if flying[slot] is not None:
                flying[slot].wait()
            stage[slot, :size, :width] = jnp.dot(
                held[i][at : at + size, :], wide[j][...], preferred_element_type=jnp.float32
            )
            flying[slot] = pltpu.make_async_copy(
                stage.at[slot, pl.ds(0, size), pl.ds(0, width)],
                out.at[pl.ds(pl.multiple_of(place[entry], 64), size), pl.ds(column, width)],
                stage_sem.at[slot],
            )
            flying[slot].start()
            turn += 1
    for copy in flying:
        if copy is not None:
            copy.wait()


def product(place, pieces, columns, pairs, out, shape, sub):
    parts = [segments for segments, _ in pieces]
    heights = [p.shape[0] for _, p in pieces]
    wides = [(own, s, c.shape[1]) for own, s, c in columns]
    epochs = columns[0][2].shape[0]
    done = sum(heights[i] * wides[j][2] for i, j in pairs)
    chained = int(out is not None)
    anywhere = pl.BlockSpec(memory_space=pl.ANY)
    args = [p for _, p in pieces] + [c for _, _, c in columns] + ([out] if chained else [])
    tall, broad = max(size for p in parts for _, size, _ in p), max(w for _, _, w in wides)
    return pl.pallas_call(
        functools.partial(product_kernel, parts, wides, pairs, sub, chained),
        grid_spec=pltpu.PrefetchScalarGridSpec(
            num_scalar_prefetch=1,
            grid=(),
            in_specs=[anywhere] * len(args),
            out_specs=anywhere,
            scratch_shapes=[pltpu.VMEM((h, epochs), jnp.bfloat16) for h in heights]
            + [pltpu.VMEM((epochs, w), jnp.bfloat16) for _, _, w in wides]
            + [
                pltpu.VMEM((3, tall, broad), jnp.float32),
                pltpu.SemaphoreType.DMA((len(heights),)),
                pltpu.SemaphoreType.DMA((len(wides),)),
                pltpu.SemaphoreType.DMA((3,)),
            ],
        ),
        out_shape=jax.ShapeDtypeStruct(shape, jnp.float32),
        input_output_aliases={len(args): 0} if chained else {},
        compiler_params=pltpu.CompilerParams(vmem_limit_bytes=VMEM_BYTES),
        cost_estimate=pl.CostEstimate(
            flops=2 * epochs * done,
            bytes_accessed=4 * done + 2 * epochs * (sum(heights) + sum(w for _, _, w in wides)),
            transcendentals=0,
        ),
        name="product",
    )(place, *args)


def tied(values, others):
    return lax.optimization_barrier((values, others))[0]


def swapped(value, axis, distance):
    return lax.ppermute(value, axis, [(i, i ^ distance) for i in range(lax.axis_size(axis))])


def share_start(index, share, sub):
    return jnp.minimum(index * share, sub - share)


def row_share(design, share):
    col_count, chips = lax.axis_size("col"), lax.axis_size("row") // 2
    row, col = lax.axis_index("row"), lax.axis_index("col")
    core, chip = lax.rem(row, 2), row // 2
    sub = design.shape[1] // 2

    def given(d):
        start = share_start(jnp.bitwise_xor(col, d), share, sub)
        return jnp.concatenate(
            [lax.dynamic_slice_in_dim(design, h * sub + start, share, 1) for h in range(2)], axis=1
        )

    panels = jnp.stack([given(0)] + [swapped(given(d), "col", d) for d in range(1, col_count)])
    held = lambda e: lax.dynamic_index_in_dim(panels, jnp.bitwise_xor(jnp.bitwise_xor(chip, e), col), 0, False)
    mine = jnp.stack([held(0)] + [swapped(held(e), "row", 2 * e) for e in range(1, chips)])
    keep = lax.dynamic_slice_in_dim(mine, core * share, share, 2)
    give = lax.dynamic_slice_in_dim(mine, (1 - core) * share, share, 2)
    return jnp.concatenate([keep, swapped(give, "row", 1)], axis=0)


def all_shares(part, first, order):
    held, away, steps = part, [0], [([order[0]], first)]
    for k, d in enumerate(order):
        new, far = (first if k == 0 else swapped(held, "col", d)), [a ^ d for a in away]
        if k > 0:
            steps.append((far, new))
        if k + 1 < len(order):
            held, away = jnp.concatenate([held, new], axis=0), away + far
    return steps


def local(design, group_ids, filter_zeros, filter_poles):
    row_count, col_count = lax.axis_size("row"), lax.axis_size("col")
    row, col = lax.axis_index("row"), lax.axis_index("col")
    core = lax.rem(row, 2)
    panel_width = design.shape[1]
    sub = panel_width // 2
    unit = sub // 13
    share = -(-sub // (128 * col_count)) * 128
    distances = [2**k for k in range((col_count - 1).bit_length())]
    starts = [share_start(jnp.bitwise_xor(col, d), share, sub) + p * (share // 2) for p in range(2) for d in range(col_count)]
    place = jnp.stack([core, row // 2] + starts).astype(jnp.int32)
    entry = lambda distance, part: 2 + part * col_count + distance
    matrix, gains = block_matrices(group_ids, filter_zeros, filter_poles, row_count)

    core_arg = core.reshape(1)
    raws, at = [], 0
    for units in COLUMN_UNITS:
        end = at + units * unit
        mine = jnp.concatenate([design[:, at:end], design[:, sub + at : sub + end]], axis=1)
        if raws:
            mine = tied(mine, matrix)
        raws.append((at, lax.all_gather(mine, "row", axis=0, tiled=True)))
        at = end

    turned = whiten_rows(place, row_share(design, share), share, matrix, gains)
    half = share // 2
    orders = [distances[p:] + distances[:p] for p in range(2)]
    parts = [turned[p * half : (p + 1) * half] for p in range(2)]
    firsts = [swapped(parts[p], "col", orders[p][0]) for p in range(2)]

    def columns_of(k, after):
        start, raw = raws[k]
        mine = whiten_columns(core_arg, tied(raw, after), COLUMN_UNITS[k] * unit, matrix, gains)
        return (True, start, mine), (False, start, swapped(mine, "row", 1))

    shape = (sub, panel_width)
    own, others = columns_of(0, turned)
    whole = ([(0, half, entry(0, 0)), (half, half, entry(0, 1))], turned)
    out = product(place, [whole], [own], [(0, 0)], None, shape, sub)
    out, firsts = lax.optimization_barrier((out, firsts))
    steps = [all_shares(parts[p], firsts[p], orders[p]) for p in range(2)]
    groups = [[whole]]
    for k in range(len(distances)):
        group = []
        for p in range(2):
            far, new = steps[p][k]
            group.append(([(s * half, half, entry(d, p)) for s, d in enumerate(far)], new))
        groups.append(group)

    early = [piece for group in groups[:-1] for piece in group]
    pairs = [(0, 1)] + [(i, j) for i in range(1, len(early)) for j in range(2)]
    out = product(place, early, [own, others], pairs, out, shape, sub)
    out, raw = lax.optimization_barrier((out, raws[1][1]))
    raws[1] = (raws[1][0], raw)
    more = columns_of(1, own[2])
    pairs = [(i, j) for j in range(2) for i in range(len(early))]
    out = product(place, early, more, pairs, out, shape, sub)
    late, every = groups[-1], [own, others, *more]
    pairs = [(i, j) for j in range(len(every)) for i in range(len(late))]
    return product(place, late, every, pairs, out, shape, sub)


def solution(mesh):
    return jax.shard_map(
        local,
        mesh=mesh,
        in_specs=(P("row", "col"), P(), P(), P()),
        out_specs=P("row", "col"),
        check_vma=False,
    )
```
